32 devices in a mesh: row: 4 (over y, x), col: 8 (over z, core).
Axes of the slice: x: 2, y: 2, z: 4, core: 2. Of those that a mesh axis runs over, the one named last changes fastest.
Arguments:
- adj_tiles: bfloat16 [4, 8, 20, 256, 256], P('row', 'col'), may hold values from -0.125 to 0.125
- tile_rows: int32 [4, 8, 20], P('row', 'col'), may hold values from 0 to 7, as said below
- tile_cols: int32 [4, 8, 20], P('row', 'col'), may hold values from 0 to 3
- tile_counts: int32 [4, 8], P('row', 'col'), may hold values from 5 to 20, as said below
- features: bfloat16 [8192, 512], P(('col', 'row')), may hold values from -6 to 6
- weight: bfloat16 [512, 512], replicated, may hold values from -0.25 to 0.25
- node_grad: bfloat16 [8192, 512], P(('row', 'col')), may hold values from -6 to 6
Outputs:
- node_out: bfloat16 [8192, 512], P(('row', 'col'))
- weight_grad: float32 [512, 512], replicated
- feature_grad: bfloat16 [8192, 512], P(('col', 'row'))
The draws below stay inside these ranges and needn't reach their ends.
Inputs may be any that keep to these rules, and one draw needn't show every extreme that they name: Within one cell the first 20 slots name distinct tiles (pairs of tile_rows and tile_cols). `tile_counts`: slots from this number on hold no tile; some cell fills all its slots.
All inputs are finite; a program needn't handle non-finite values.
Results may differ from the reference program's by a relative error of at most 0.027.
Values may be sent and summed in bfloat16 or wider, within the bound.
A program may use at most 128 MiB of HBM per device.

```python
import jax
import jax.numpy as jnp
from jax import lax

F = 512
H = 512
TILE = 256
GRID_R = 4
GRID_C = 8
NODES = 8192
TROW = 8
TCOL = 4
TMAX = 20
TMIN = 5
N_COL = 8


def cell_positions(key):
    base = jax.random.fold_in(key, 11)
    cell_keys = jax.random.split(base, GRID_R * GRID_C)

    def pick_cell(cell_key):
        return jax.random.permutation(cell_key, TROW * TCOL)[:TMAX]
    picks = jax.vmap(pick_cell)(cell_keys)
    return picks.reshape(GRID_R, GRID_C, TMAX).astype(jnp.int32)


def draw_tile_rows(key, part):
    return cell_positions(key) // TCOL


def draw_tile_cols(key, part):
    return cell_positions(key) % TCOL


def draw_tile_counts(key, part):
    first_key, second_key = jax.random.split(jax.random.fold_in(key, 23))
    level = jax.random.randint(first_key, (GRID_R * GRID_C,), 0, 8)
    counts = TMIN + level * level * (TMAX - TMIN) // 49
    heavy = jax.random.randint(second_key, (), 0, GRID_R * GRID_C)
    places = jnp.arange(GRID_R * GRID_C)
    counts = jnp.where(places == heavy, TMAX, counts)
    return counts.reshape(GRID_R, GRID_C).astype(jnp.int32)


def levels(key, extent, cuts, least, largest):
    gain = 1.0
    for position, blocks in cuts:
        steps = jax.random.uniform(jax.random.fold_in(jax.random.fold_in(key, 6), position), (blocks,), jnp.float32, least / len(cuts), largest / len(cuts))
        gain = gain * jnp.repeat(jnp.exp(steps), extent[position] // blocks).reshape((-1,) + (1,) * (len(extent) - 1 - position))
    return gain


def scatter_about(rng, extent, deviation, most, cuts=(), kind=jnp.bfloat16):
    gain = levels(rng, extent, cuts, -0.22, 0.18) if cuts else 1.0
    drawn = jax.random.normal(rng, extent, jnp.float32) * deviation * gain
    return jnp.minimum(jnp.maximum(drawn, -most), most).astype(kind)


def setup_inputs(seed: int = 0) -> dict:
    splits = jax.random.split(jax.random.key(seed), 8)
    return {
        "adj_tiles": scatter_about(splits[0], (GRID_R, GRID_C, TMAX, TILE, TILE), (TILE * N_COL * TMAX // (2 * TROW)) ** -0.5, 0.125, ((0, 4), (1, 8))),
        "tile_rows": draw_tile_rows(jax.random.fold_in(splits[7], 71), 0),
        "tile_cols": draw_tile_cols(jax.random.fold_in(splits[7], 71), 0),
        "tile_counts": draw_tile_counts(jax.random.fold_in(splits[7], 71), 0),
        "features": scatter_about(splits[4], (NODES, F), 1.0, 6.0, ((0, 32),)),
        "weight": scatter_about(splits[5], (F, H), F ** -0.5, 0.25),
        "node_grad": scatter_about(splits[6], (NODES, H), 1.0, 6.0, ((0, 32),)),
    }


def cell_forward(cell_tiles, cell_rows, cell_cols, cell_count, source):
    total = jnp.zeros((TROW, TILE, F), jnp.float32)

    def add_tile(slot, running):
        tile = lax.dynamic_index_in_dim(cell_tiles, slot, 0, False)
        block = lax.dynamic_index_in_dim(source, cell_cols[slot], 0, False)
        product = jnp.dot(tile, block, preferred_element_type=jnp.float32)
        return running.at[cell_rows[slot]].add(product)
    return lax.fori_loop(jnp.int32(0), cell_count.astype(jnp.int32), add_tile, total)

def cell_backward(cell_tiles, cell_rows, cell_cols, cell_count, source):
    total = jnp.zeros((TCOL, TILE, F), jnp.float32)

    def add_tile(slot, running):
        tile = lax.dynamic_index_in_dim(cell_tiles, slot, 0, False)
        block = lax.dynamic_index_in_dim(source, cell_rows[slot], 0, False)
        product = jnp.dot(tile.T, block, preferred_element_type=jnp.float32)
        return running.at[cell_cols[slot]].add(product)
    return lax.fori_loop(jnp.int32(0), cell_count.astype(jnp.int32), add_tile, total)

def rounded(values):
    return lax.optimization_barrier(values.astype(jnp.bfloat16)).astype(jnp.float32)

def reference(adj_tiles, tile_rows, tile_cols, tile_counts, features, weight, node_grad):
    column_feats = features.reshape(GRID_C, TCOL, TILE, F)

    def row_block(row_index):

        def add_cell(col_index, running):
            part = cell_forward(adj_tiles[row_index, col_index], tile_rows[row_index, col_index], tile_cols[row_index, col_index], tile_counts[row_index, col_index], column_feats[col_index])
            return running + rounded(part)
        return lax.fori_loop(0, GRID_C, add_cell, jnp.zeros((TROW, TILE, F), jnp.float32))
    agg = lax.map(row_block, jnp.arange(GRID_R, dtype=jnp.int32)).reshape(NODES, F)
    agg_b = agg.astype(jnp.bfloat16)
    pre = jnp.dot(agg_b, weight, preferred_element_type=jnp.float32)
    node_out = jax.nn.silu(pre).astype(jnp.bfloat16)
    sigma = jax.nn.sigmoid(pre)
    dpre = (node_grad.astype(jnp.float32) * sigma * (1.0 + pre * (1.0 - sigma))).astype(jnp.bfloat16)
    weight_grad = jnp.dot(agg_b.T, dpre, preferred_element_type=jnp.float32) / jnp.sqrt(jnp.float32(NODES))
    dagg = jnp.dot(dpre, weight.T, preferred_element_type=jnp.float32).astype(jnp.bfloat16)
    grad_blocks = dagg.reshape(GRID_R, TROW, TILE, F)

    def col_block(col_index):

        def add_cell(row_index, running):
            part = cell_backward(adj_tiles[row_index, col_index], tile_rows[row_index, col_index], tile_cols[row_index, col_index], tile_counts[row_index, col_index], grad_blocks[row_index])
            return running + rounded(part)
        return lax.fori_loop(0, GRID_R, add_cell, jnp.zeros((TCOL, TILE, F), jnp.float32))
    feature_grad = lax.map(col_block, jnp.arange(GRID_C, dtype=jnp.int32)).reshape(NODES, F).astype(jnp.bfloat16)
    return (node_out, weight_grad, feature_grad)
```

```python
import functools

import jax
import jax.numpy as jnp
from jax import lax
from jax.experimental import pallas as pl
from jax.experimental.pallas import tpu as pltpu
from jax.sharding import PartitionSpec as P

BF = jnp.bfloat16
F32 = jnp.float32
HALVES = 2


def dot(a, b):
    return jnp.dot(a, b, preferred_element_type=F32)


def kernel(
    R,
    C,
    scale,
    rows_s,
    cols_s,
    count_s,
    adj_hbm,
    feat,
    weight,
    ngrad,
    out,
    wout,
    fgrad,
    adj,
    place,
    denseT,
    feats,
    chip,
    sib_send,
    sib_recv,
    up_recv,
    dn_recv,
    agg,
    dpre_v,
    grads,
    b_send,
    b_recv,
    wterm,
    w1_send,
    w1_recv,
    w1_sum,
    w2_send,
    w2_recv,
    wslab,
    wfull,
    adj_sem,
    f_s,
    f_r,
    sib_s,
    sib_r,
    up_s,
    up_r,
    dn_s,
    dn_r,
    gsib_s,
    gsib_r,
    gup_s,
    gup_r,
    gdn_s,
    gdn_r,
    b_s,
    b_r,
    w1_s,
    w1_r,
    w2_s,
    w2_r,
    w3_s,
    w3_r,
    w4_s,
    w4_r,
):
    H = HALVES
    Z = C // 2
    T, F = feat.shape
    W = F // H
    slots = adj.shape[0] - 1
    i = lax.axis_index("row")
    j = lax.axis_index("col")
    z = j // 2
    c = lax.rem(j, 2)
    sibling = 2 * z + 1 - c
    pending = []

    def remote(src, dst, ssem, rsem, row, col):
        return pltpu.make_async_remote_copy(
            src_ref=src,
            dst_ref=dst,
            send_sem=ssem,
            recv_sem=rsem,
            device_id=(row, col),
            device_id_type=pl.DeviceIdType.MESH,
        )

    def send(copy, cond=None):
        if cond is None:
            copy.start()
        else:
            pl.when(cond)(copy.start)
        pending.append((copy, cond))

    adj_copy = pltpu.make_async_copy(adj_hbm.at[0, 0], adj.at[pl.ds(0, slots)], adj_sem)
    adj_copy.start()

    barrier = pltpu.get_barrier_semaphore()
    for q in range(1, R):
        pl.semaphore_signal(
            barrier, inc=1, device_id=(lax.rem(i + q, R), j), device_id_type=pl.DeviceIdType.MESH
        )
    for q in range(1, C):
        pl.semaphore_signal(
            barrier, inc=1, device_id=(i, lax.rem(j + q, C)), device_id_type=pl.DeviceIdType.MESH
        )
    pl.semaphore_wait(barrier, R + C - 2)

    def tile_at(index):
        return pl.ds(pl.multiple_of(index * T, T), T)

    def feat_copy(h, q):
        return remote(
            feat.at[:, pl.ds(h * W, W)],
            feats.at[h, tile_at(i), :],
            f_s.at[h, q - 1],
            f_r.at[h, q - 1],
            lax.rem(i + q, R),
            j,
        )

    for h in range(H):
        for q in range(1, R):
            send(feat_copy(h, q))
    for h in range(H):
        feats[h, tile_at(i), :] = feat[:, pl.ds(h * W, W)]

    adj[slots] = jnp.zeros((T, T), BF)
    adj_copy.wait()
    count = count_s[0, 0]

    def fill(r, carry):
        for k in range(R):
            found = jnp.int32(slots)
            for t in range(slots):
                hit = (rows_s[0, 0, t] == r) & (cols_s[0, 0, t] == k) & (t < count)
                found = jnp.where(hit, jnp.int32(t), found)
            place[r * R + k] = found
            denseT[k, :, tile_at(r)] = adj[found].T
        return carry

    lax.fori_loop(0, C, fill, 0)

    order = []
    for s in range((Z + 1) // 2):
        order.append(Z - 1 - s)
        if s != Z - 1 - s:
            order.append(s)

    def sib_copy(h, d):
        return remote(
            sib_send.at[h, d], sib_recv.at[h, d], sib_s.at[h, d], sib_r.at[h, d], i, sibling
        )

    def cell_rows(h, r):
        acc = dot(adj[place[r * R]], feats[h, :T, :])
        for k in range(1, R):
            acc = acc + dot(adj[place[r * R + k]], feats[h, k * T : (k + 1) * T, :])
        return acc

    def forward(h):
        for q in range(1, R):
            feat_copy(h, q).wait_recv()
        for d in order:
            sib_send[h, d] = cell_rows(h, 2 * d + 1 - c).astype(BF)
            send(sib_copy(h, d))
        for d in order:
            part = cell_rows(h, 2 * d + c)
            sib_copy(h, d).wait_recv()
            chip[h, d] = (part + sib_recv[h, d].astype(F32)).astype(BF)

    above = jnp.minimum(z + 1, Z - 1)
    below = jnp.maximum(z - 1, 0)

    def up_copy(h, s):
        return remote(
            chip.at[h, Z - 1 - s], up_recv.at[h, s], up_s.at[h, s], up_r.at[h, s], i, 2 * above + c
        )

    def dn_copy(h, s):
        return remote(
            chip.at[h, s], dn_recv.at[h, s], dn_s.at[h, s], dn_r.at[h, s], i, 2 * below + c
        )

    def chain(h, s):
        d = Z - 1 - s

        @pl.when((z > 0) & (z < d))
        def _():
            up_copy(h, s).wait_recv()
            chip[h, d] = (chip[h, d].astype(F32) + up_recv[h, s].astype(F32)).astype(BF)

        send(up_copy(h, s), z < d)

        @pl.when((z < Z - 1) & (z > s))
        def _():
            dn_copy(h, s).wait_recv()
            chip[h, s] = (chip[h, s].astype(F32) + dn_recv[h, s].astype(F32)).astype(BF)

        send(dn_copy(h, s), z > s)

    def finish(h):
        cols = pl.ds(h * W, W)

        @pl.when(z == 0)
        def _():
            dn_copy(h, z).wait_recv()
            agg[:, cols] = (chip[h, z].astype(F32) + dn_recv[h, z].astype(F32)).astype(BF)

        @pl.when(z == Z - 1)
        def _():
            up_copy(h, Z - 1 - z).wait_recv()
            agg[:, cols] = (chip[h, z].astype(F32) + up_recv[h, Z - 1 - z].astype(F32)).astype(BF)

        @pl.when((z > 0) & (z < Z - 1))
        def _():
            up_copy(h, Z - 1 - z).wait_recv()
            dn_copy(h, z).wait_recv()
            both = up_recv[h, Z - 1 - z].astype(F32) + dn_recv[h, z].astype(F32)
            agg[:, cols] = (chip[h, z].astype(F32) + both).astype(BF)

    forward(0)
    for s in range(Z - 2):
        chain(0, s)
    forward(1)
    chain(1, 0)
    chain(0, Z - 2)
    for s in range(1, Z - 1):
        chain(1, s)
    finish(0)
    finish(1)

    pre = dot(agg[...], weight[...])
    sigma = 1.0 / (1.0 + jnp.exp(-pre))
    dpre = (ngrad[...].astype(F32) * sigma * (1.0 + pre * (1.0 - sigma))).astype(BF)
    dpre_v[...] = dpre
    out[...] = (pre * sigma).astype(BF)

    def gsib_copy(h, owner):
        rows = tile_at(2 * owner + c)
        return remote(
            grads.at[h, rows, :], grads.at[h, rows, :], gsib_s.at[h, owner], gsib_r.at[h, owner],
            i, sibling,
        )

    def gup_copy(h, s):
        rows = tile_at(2 * jnp.maximum(z - s, 0) + c)
        return remote(
            grads.at[h, rows, :], grads.at[h, rows, :], gup_s.at[h, s], gup_r.at[h, s],
            i, 2 * above + c,
        )

    def gdn_copy(h, s):
        rows = tile_at(2 * jnp.minimum(z + s, Z - 1) + c)
        return remote(
            grads.at[h, rows, :], grads.at[h, rows, :], gdn_s.at[h, s], gdn_r.at[h, s],
            i, 2 * below + c,
        )

    for h in range(H):
        part = lax.dot_general(
            dpre_v[...],
            weight[h * W : (h + 1) * W, :],
            (((1,), (1,)), ((), ())),
            preferred_element_type=F32,
        )
        grads[h, tile_at(j), :] = part.astype(BF)
        send(gup_copy(h, 0), z < Z - 1)
        send(gdn_copy(h, 0), z > 0)
        send(gsib_copy(h, z))

    S1 = F // R
    groups = S1 // 16
    cg = C // groups
    width = F // cg

    def slab_at(index):
        return pl.ds(pl.multiple_of(index * S1, S1), S1)

    def piece_at(index):
        return (
            pl.ds(pl.multiple_of(index // cg * 16, 16), 16),
            pl.ds(pl.multiple_of(lax.rem(index, cg) * width, width), width),
        )

    def w1_copy(q):
        return remote(
            w1_send.at[q - 1], w1_recv.at[q - 1], w1_s.at[q - 1], w1_r.at[q - 1],
            lax.rem(i + q, R), j,
        )

    def w2_copy(q):
        return remote(
            w2_send.at[q - 1], w2_recv.at[q - 1], w2_s.at[q - 1], w2_r.at[q - 1],
            i, lax.rem(j + q, C),
        )

    def w3_copy(q, owner):
        r, k = piece_at(owner)
        return remote(
            wslab.at[r, k], wslab.at[r, k], w3_s.at[q - 1], w3_r.at[q - 1], i, lax.rem(j + q, C)
        )

    def w4_copy(q, owner):
        rows = slab_at(owner)
        return remote(
            wslab, wfull.at[rows, :], w4_s.at[q - 1], w4_r.at[q - 1], lax.rem(i + q, R), j
        )

    wterm[...] = (
        lax.dot_general(
            agg[...], dpre_v[...], (((0,), (0,)), ((), ())), preferred_element_type=F32
        )
        * scale
    )
    for q in range(1, R):
        w1_send[q - 1] = wterm[slab_at(lax.rem(i + q, R)), :].astype(BF)
        send(w1_copy(q))

    def gather(h, s):
        from_below = z - 1 - s >= 0
        from_above = z + 1 + s <= Z - 1

        @pl.when(from_below)
        def _():
            gup_copy(h, s).wait_recv()

        if s + 1 < Z - 1:
            send(gup_copy(h, s + 1), from_below & (z < Z - 1))
        send(gsib_copy(h, jnp.maximum(z - 1 - s, 0)), from_below)

        @pl.when(from_above)
        def _():
            gdn_copy(h, s).wait_recv()

        if s + 1 < Z - 1:
            send(gdn_copy(h, s + 1), from_above & (z > 0))
        send(gsib_copy(h, jnp.minimum(z + 1 + s, Z - 1)), from_above)

    def b_copy(h, q):
        return remote(
            b_send.at[h, q - 1], b_recv.at[h, q - 1], b_s.at[h, q - 1], b_r.at[h, q - 1],
            lax.rem(i + q, R), j,
        )

    def backward(h):
        for d in range(Z):
            gsib_copy(h, d).wait_recv()
        for q in range(1, R):
            b_send[h, q - 1] = dot(denseT[lax.rem(i + q, R)], grads[h]).astype(BF)
            send(b_copy(h, q))

    def total(h):
        acc = dot(denseT[i], grads[h])
        for q in range(1, R):
            b_copy(h, q).wait_recv()
            acc = acc + b_recv[h, q - 1].astype(F32)
        fgrad[:, h * W : (h + 1) * W] = acc.astype(BF)

    gather(0, 0)
    gather(1, 0)
    acc = wterm[slab_at(i), :]
    for q in range(1, R):
        w1_copy(q).wait_recv()
        acc = acc + w1_recv[q - 1].astype(F32)
    w1_sum[...] = acc
    for q in range(1, C):
        r, k = piece_at(lax.rem(j + q, C))
        w2_send[q - 1] = w1_sum[r, k].astype(BF)
        send(w2_copy(q))
    gather(0, 1)
    gather(1, 1)
    r, k = piece_at(j)
    acc = w1_sum[r, k]
    for q in range(1, C):
        w2_copy(q).wait_recv()
        acc = acc + w2_recv[q - 1].astype(F32)
    wslab[r, k] = acc.astype(BF)
    for q in range(1, C):
        send(w3_copy(q, j))
    for s in range(2, Z - 1):
        gather(0, s)
        gather(1, s)
    backward(0)
    for q in range(1, C):
        w3_copy(q, lax.rem(j - q + C, C)).wait_recv()
    backward(1)
    for q in range(1, R):
        send(w4_copy(q, i))
    wfull[slab_at(i), :] = wslab[...]
    total(0)
    total(1)
    for q in range(1, R):
        w4_copy(q, lax.rem(i - q + R, R)).wait_recv()
    wout[...] = wfull[...].astype(F32)

    for copy, cond in pending:
        if cond is None:
            copy.wait_send()
        else:
            pl.when(cond)(copy.wait_send)


def local(adj_tiles, tile_rows, tile_cols, tile_counts, features, weight, node_grad):
    R = lax.axis_size("row")
    C = lax.axis_size("col")
    Z = C // 2
    H = HALVES
    T, F = features.shape
    W = F // H
    slots = adj_tiles.shape[2]
    S1 = F // R
    width = F // (C // (S1 // 16))
    scale = float((T * R * C) ** -0.5)
    vmem = pltpu.VMEM
    dma = pltpu.SemaphoreType.DMA
    scratch = [
        vmem((slots + 1, T, T), BF),
        pltpu.SMEM((C * R,), jnp.int32),
        vmem((R, T, C * T), BF),
        vmem((H, R * T, W), BF),
        vmem((H, Z, T, W), BF),
        vmem((H, Z, T, W), BF),
        vmem((H, Z, T, W), BF),
        vmem((H, Z - 1, T, W), BF),
        vmem((H, Z - 1, T, W), BF),
        vmem((T, F), BF),
        vmem((T, F), BF),
        vmem((H, C * T, W), BF),
        vmem((H, R - 1, T, W), BF),
        vmem((H, R - 1, T, W), BF),
        vmem((F, F), F32),
        vmem((R - 1, S1, F), BF),
        vmem((R - 1, S1, F), BF),
        vmem((S1, F), F32),
        vmem((C - 1, 16, width), BF),
        vmem((C - 1, 16, width), BF),
        vmem((S1, F), BF),
        vmem((F, F), BF),
        dma(()),
    ]
    for shape in (
        (H, R - 1),
        (H, Z),
        (H, Z - 1),
        (H, Z - 1),
        (H, Z),
        (H, Z - 1),
        (H, Z - 1),
        (H, R - 1),
        (R - 1,),
        (C - 1,),
        (C - 1,),
        (R - 1,),
    ):
        scratch += [dma(shape), dma(shape)]
    whole = pl.BlockSpec(memory_space=pltpu.VMEM)
    scalars = pl.BlockSpec(memory_space=pltpu.SMEM)
    return pl.pallas_call(
        functools.partial(kernel, R, C, scale),
        out_shape=(
            jax.ShapeDtypeStruct((T, F), BF),
            jax.ShapeDtypeStruct((F, F), F32),
            jax.ShapeDtypeStruct((T, F), BF),
        ),
        in_specs=[scalars] * 3 + [pl.BlockSpec(memory_space=pl.ANY)] + [whole] * 3,
        out_specs=(whole, whole, whole),
        scratch_shapes=scratch,
        compiler_params=pltpu.CompilerParams(
            collective_id=0, has_side_effects=True, vmem_limit_bytes=60 * 1024 * 1024
        ),
        name="layer",
    )(tile_rows, tile_cols, tile_counts, adj_tiles, features, weight, node_grad)


def solution(mesh):
    in_specs = (
        P("row", "col", None, None, None),
        P("row", "col", None),
        P("row", "col", None),
        P("row", "col"),
        P(("col", "row"), None),
        P(),
        P(("row", "col"), None),
    )
    out_specs = (P(("row", "col"), None), P(), P(("col", "row"), None))
    return jax.shard_map(local, mesh=mesh, in_specs=in_specs, out_specs=out_specs, check_vma=False)
```

```python
import functools

import jax
import jax.numpy as jnp
from jax import lax
from jax.experimental import pallas as pl
from jax.experimental.pallas import tpu as pltpu
from jax.sharding import PartitionSpec as P

BF = jnp.bfloat16
F32 = jnp.float32
HALVES = 2


def dot(a, b):
    return jnp.dot(a, b, preferred_element_type=F32)


def kernel(
    R,
    C,
    scale,
    rows_s,
    cols_s,
    count_s,
    adj_hbm,
    feat,
    weight,
    ngrad,
    out,
    wfull,
    fgrad,
    adj,
    place,
    feats,
    chip,
    sib_send,
    sib_recv,
    up_recv,
    dn_recv,
    agg,
    dpre_v,
    grads,
    b_send,
    b_recv,
    wterm,
    w0_send,
    w0_recv,
    w_pair,
    w1_send,
    w1_recv,
    w1_sum,
    w2_send,
    w2_recv,
    wslab,
    adj_sem,
    f_s,
    f_r,
    sib_s,
    sib_r,
    up_s,
    up_r,
    dn_s,
    dn_r,
    gsib_s,
    gsib_r,
    gup_s,
    gup_r,
    gdn_s,
    gdn_r,
    b_s,
    b_r,
    w0_s,
    w0_r,
    w1_s,
    w1_r,
    w2_s,
    w2_r,
    w3_s,
    w3_r,
    w4_s,
    w4_r,
    w5_s,
    w5_r,
):
    H = HALVES
    Z = C // 2
    T, F = feat.shape
    W = F // H
    slots = adj.shape[0] - 1
    i = lax.axis_index("row")
    j = lax.axis_index("col")
    z = j // 2
    c = lax.rem(j, 2)
    sibling = 2 * z + 1 - c
    pending = []

    def remote(src, dst, ssem, rsem, row, col):
        return pltpu.make_async_remote_copy(
            src_ref=src,
            dst_ref=dst,
            send_sem=ssem,
            recv_sem=rsem,
            device_id=(row, col),
            device_id_type=pl.DeviceIdType.MESH,
        )

    def send(copy, cond=None):
        if cond is None:
            copy.start()
        else:
            pl.when(cond)(copy.start)
        pending.append((copy, cond))

    adj_copy = pltpu.make_async_copy(adj_hbm.at[0, 0], adj.at[pl.ds(0, slots)], adj_sem)
    adj_copy.start()

    barrier = pltpu.get_barrier_semaphore()
    for q in range(1, R):
        pl.semaphore_signal(
            barrier, inc=1, device_id=(lax.rem(i + q, R), j), device_id_type=pl.DeviceIdType.MESH
        )
    for q in range(1, C):
        pl.semaphore_signal(
            barrier, inc=1, device_id=(i, lax.rem(j + q, C)), device_id_type=pl.DeviceIdType.MESH
        )
    pl.semaphore_wait(barrier, R + C - 2)

    def tile_at(index):
        return pl.ds(pl.multiple_of(index * T, T), T)

    def feat_copy(h, q):
        return remote(
            feat.at[:, pl.ds(h * W, W)],
            feats.at[h, tile_at(i), :],
            f_s.at[h, q - 1],
            f_r.at[h, q - 1],
            lax.rem(i + q, R),
            j,
        )

    for h in range(H):
        for q in range(1, R):
            send(feat_copy(h, q))
    for h in range(H):
        feats[h, tile_at(i), :] = feat[:, pl.ds(h * W, W)]

    adj[slots] = jnp.zeros((T, T), BF)
    adj_copy.wait()
    count = count_s[0, 0]

    def fill(r, carry):
        for k in range(R):
            found = jnp.int32(slots)
            for t in range(slots):
                hit = (rows_s[0, 0, t] == r) & (cols_s[0, 0, t] == k) & (t < count)
                found = jnp.where(hit, jnp.int32(t), found)
            place[r * R + k] = found
        return carry

    lax.fori_loop(0, C, fill, 0)

    order = []
    for s in range((Z + 1) // 2):
        order.append(Z - 1 - s)
        if s != Z - 1 - s:
            order.append(s)

    def sib_copy(h, d):
        return remote(
            sib_send.at[h, d], sib_recv.at[h, d], sib_s.at[h, d], sib_r.at[h, d], i, sibling
        )

    def cell_rows(h, r):
        acc = dot(adj[place[r * R]], feats[h, :T, :])
        for k in range(1, R):
            acc = acc + dot(adj[place[r * R + k]], feats[h, k * T : (k + 1) * T, :])
        return acc

    def forward(h):
        for q in range(1, R):
            feat_copy(h, q).wait_recv()
        for d in order:
            sib_send[h, d] = cell_rows(h, 2 * d + 1 - c).astype(BF)
            send(sib_copy(h, d))
        for d in order:
            part = cell_rows(h, 2 * d + c)
            sib_copy(h, d).wait_recv()
            chip[h, d] = (part + sib_recv[h, d].astype(F32)).astype(BF)

    above = jnp.minimum(z + 1, Z - 1)
    below = jnp.maximum(z - 1, 0)

    def up_copy(h, s):
        return remote(
            chip.at[h, Z - 1 - s], up_recv.at[h, s], up_s.at[h, s], up_r.at[h, s], i, 2 * above + c
        )

    def dn_copy(h, s):
        return remote(
            chip.at[h, s], dn_recv.at[h, s], dn_s.at[h, s], dn_r.at[h, s], i, 2 * below + c
        )

    def chain(h, s):
        d = Z - 1 - s

        @pl.when((z > 0) & (z < d))
        def _():
            up_copy(h, s).wait_recv()
            chip[h, d] = (chip[h, d].astype(F32) + up_recv[h, s].astype(F32)).astype(BF)

        send(up_copy(h, s), z < d)

        @pl.when((z < Z - 1) & (z > s))
        def _():
            dn_copy(h, s).wait_recv()
            chip[h, s] = (chip[h, s].astype(F32) + dn_recv[h, s].astype(F32)).astype(BF)

        send(dn_copy(h, s), z > s)

    def finish(h):
        cols = pl.ds(h * W, W)

        @pl.when(z == 0)
        def _():
            dn_copy(h, z).wait_recv()
            agg[:, cols] = (chip[h, z].astype(F32) + dn_recv[h, z].astype(F32)).astype(BF)

        @pl.when(z == Z - 1)
        def _():
            up_copy(h, Z - 1 - z).wait_recv()
            agg[:, cols] = (chip[h, z].astype(F32) + up_recv[h, Z - 1 - z].astype(F32)).astype(BF)

        @pl.when((z > 0) & (z < Z - 1))
        def _():
            up_copy(h, Z - 1 - z).wait_recv()
            dn_copy(h, z).wait_recv()
            both = up_recv[h, Z - 1 - z].astype(F32) + dn_recv[h, z].astype(F32)
            agg[:, cols] = (chip[h, z].astype(F32) + both).astype(BF)

    forward(0)
    for s in range(Z - 2):
        chain(0, s)
    forward(1)
    chain(1, 0)
    chain(0, Z - 2)
    for s in range(1, Z - 1):
        chain(1, s)
    finish(0)
    finish(1)

    pre = dot(agg[...], weight[...])
    sigma = 1.0 / (1.0 + jnp.exp(-pre))
    dpre = (ngrad[...].astype(F32) * sigma * (1.0 + pre * (1.0 - sigma))).astype(BF)
    dpre_v[...] = dpre

    def gsib_copy(h, owner):
        r = 2 * owner + c
        return remote(
            grads.at[h, r], grads.at[h, r], gsib_s.at[h, owner], gsib_r.at[h, owner],
            i, sibling,
        )

    def gup_copy(h, s):
        r = 2 * jnp.maximum(z - s, 0) + c
        return remote(
            grads.at[h, r], grads.at[h, r], gup_s.at[h, s], gup_r.at[h, s],
            i, 2 * above + c,
        )

    def gdn_copy(h, s):
        r = 2 * jnp.minimum(z + s, Z - 1) + c
        return remote(
            grads.at[h, r], grads.at[h, r], gdn_s.at[h, s], gdn_r.at[h, s],
            i, 2 * below + c,
        )

    for h in range(H):
        part = lax.dot_general(
            weight[h * W : (h + 1) * W, :],
            dpre_v[...],
            (((1,), (1,)), ((), ())),
            preferred_element_type=F32,
        )
        grads[h, j] = part.astype(BF)
        send(gup_copy(h, 0), z < Z - 1)
        send(gdn_copy(h, 0), z > 0)
        send(gsib_copy(h, z))

    out[...] = (pre * sigma).astype(BF)

    half = F // 2
    S1 = half // R
    groups = S1 // 16
    cg = Z // groups
    width = F // cg

    def slab_at(index):
        return pl.ds(pl.multiple_of(index * S1, S1), S1)

    def half_at(index):
        return pl.ds(pl.multiple_of(index * half, half), half)

    def piece_at(index):
        return (
            pl.ds(pl.multiple_of(index // cg * 16, 16), 16),
            pl.ds(pl.multiple_of(lax.rem(index, cg) * width, width), width),
        )

    w0_copy = remote(w0_send, w0_recv, w0_s, w0_r, i, sibling)

    def w1_copy(q):
        return remote(
            w1_send.at[q - 1], w1_recv.at[q - 1], w1_s.at[q - 1], w1_r.at[q - 1],
            lax.rem(i + q, R), j,
        )

    def w2_copy(q):
        return remote(
            w2_send.at[q - 1], w2_recv.at[q - 1], w2_s.at[q - 1], w2_r.at[q - 1],
            i, 2 * lax.rem(z + q, Z) + c,
        )

    def w3_copy(q, owner):
        r, k = piece_at(owner)
        return remote(
            wslab.at[r, k], wslab.at[r, k], w3_s.at[q - 1], w3_r.at[q - 1],
            i, 2 * lax.rem(z + q, Z) + c,
        )

    def w4_copy(q, owner):
        rows = slab_at(c * R + owner)
        return remote(
            wslab, wfull.at[rows, :], w4_s.at[q - 1], w4_r.at[q - 1], lax.rem(i + q, R), j
        )

    def w5_copy(core):
        rows = half_at(core)
        return remote(wfull.at[rows, :], wfull.at[rows, :], w5_s, w5_r, i, sibling)

    wterm[...] = (
        lax.dot_general(
            agg[...], dpre_v[...], (((0,), (0,)), ((), ())), preferred_element_type=F32
        )
        * scale
    )
    w0_send[...] = wterm[half_at(1 - c), :].astype(BF)
    send(w0_copy)

    def sum_pair():
        w0_copy.wait_recv()
        w_pair[...] = wterm[half_at(c), :] + w0_recv[...].astype(F32)
        for q in range(1, R):
            w1_send[q - 1] = w_pair[slab_at(lax.rem(i + q, R)), :].astype(BF)
            send(w1_copy(q))

    def sum_row():
        acc = w_pair[slab_at(i), :]
        for q in range(1, R):
            w1_copy(q).wait_recv()
            acc = acc + w1_recv[q - 1].astype(F32)
        w1_sum[...] = acc
        for q in range(1, Z):
            r, k = piece_at(lax.rem(z + q, Z))
            w2_send[q - 1] = w1_sum[r, k].astype(BF)
            send(w2_copy(q))

    def sum_chain():
        r, k = piece_at(z)
        acc = w1_sum[r, k]
        for q in range(1, Z):
            w2_copy(q).wait_recv()
            acc = acc + w2_recv[q - 1].astype(F32)
        wslab[r, k] = acc.astype(BF)
        for q in range(1, Z):
            send(w3_copy(q, z))

    def share_row():
        for q in range(1, Z):
            w3_copy(q, lax.rem(z - q + Z, Z)).wait_recv()
        for q in range(1, R):
            send(w4_copy(q, i))
        wfull[slab_at(c * R + i), :] = wslab[...]

    def share_pair():
        for q in range(1, R):
            w4_copy(q, lax.rem(i - q + R, R)).wait_recv()
        send(w5_copy(c))

    def gather(h, s):
        from_below = z - 1 - s >= 0
        from_above = z + 1 + s <= Z - 1

        @pl.when(from_below)
        def _():
            gup_copy(h, s).wait_recv()

        if s + 1 < Z - 1:
            send(gup_copy(h, s + 1), from_below & (z < Z - 1))
        send(gsib_copy(h, jnp.maximum(z - 1 - s, 0)), from_below)

        @pl.when(from_above)
        def _():
            gdn_copy(h, s).wait_recv()

        if s + 1 < Z - 1:
            send(gdn_copy(h, s + 1), from_above & (z > 0))
        send(gsib_copy(h, jnp.minimum(z + 1 + s, Z - 1)), from_above)

    def b_copy(h, q):
        return remote(
            b_send.at[h, q - 1], b_recv.at[h, q - 1], b_s.at[h, q - 1], b_r.at[h, q - 1],
            lax.rem(i + q, R), j,
        )

    def cell_cols(h, k):
        acc = dot(grads[h, 0], adj[place[k]])
        for r in range(1, C):
            acc = acc + dot(grads[h, r], adj[place[r * R + k]])
        return acc

    def backward(h):
        for d in range(Z):
            gsib_copy(h, d).wait_recv()
        for q in range(1, R):
            b_send[h, q - 1] = cell_cols(h, lax.rem(i + q, R)).astype(BF)
            send(b_copy(h, q))

    def total(h):
        acc = cell_cols(h, i)
        for q in range(1, R):
            b_copy(h, q).wait_recv()
            acc = acc + b_recv[h, q - 1].astype(F32)
        fgrad[:, h * W : (h + 1) * W] = acc.T.astype(BF)

    gather(0, 0)
    sum_pair()
    gather(0, 1)
    gather(1, 0)
    sum_row()
    for s in range(2, Z - 1):
        gather(0, s)
        gather(1, s - 1)
    backward(0)
    sum_chain()
    gather(1, Z - 2)
    share_row()
    backward(1)
    total(0)
    share_pair()
    total(1)
    w5_copy(1 - c).wait_recv()

    for copy, cond in pending:
        if cond is None:
            copy.wait_send()
        else:
            pl.when(cond)(copy.wait_send)


def hand_over(node_in, weight_in, feature_in, node_out, weight_out, feature_out):
    node_out[...] = node_in[...]
    weight_out[...] = weight_in[...].astype(F32)
    feature_out[...] = feature_in[...]


def local(adj_tiles, tile_rows, tile_cols, tile_counts, features, weight, node_grad):
    R = lax.axis_size("row")
    C = lax.axis_size("col")
    Z = C // 2
    H = HALVES
    T, F = features.shape
    W = F // H
    slots = adj_tiles.shape[2]
    S1 = F // 2 // R
    width = F // (Z // (S1 // 16))
    scale = float((T * R * C) ** -0.5)
    vmem = pltpu.VMEM
    dma = pltpu.SemaphoreType.DMA
    scratch = [
        vmem((slots + 1, T, T), BF),
        pltpu.SMEM((C * R,), jnp.int32),
        vmem((H, R * T, W), BF),
        vmem((H, Z, T, W), BF),
        vmem((H, Z, T, W), BF),
        vmem((H, Z, T, W), BF),
        vmem((H, Z - 1, T, W), BF),
        vmem((H, Z - 1, T, W), BF),
        vmem((T, F), BF),
        vmem((T, F), BF),
        vmem((H, C, W, T), BF),
        vmem((H, R - 1, W, T), BF),
        vmem((H, R - 1, W, T), BF),
        vmem((F, F), F32),
        vmem((F // 2, F), BF),
        vmem((F // 2, F), BF),
        vmem((F // 2, F), F32),
        vmem((R - 1, S1, F), BF),
        vmem((R - 1, S1, F), BF),
        vmem((S1, F), F32),
        vmem((Z - 1, 16, width), BF),
        vmem((Z - 1, 16, width), BF),
        vmem((S1, F), BF),
        dma(()),
    ]
    for shape in (
        (H, R - 1),
        (H, Z),
        (H, Z - 1),
        (H, Z - 1),
        (H, Z),
        (H, Z - 1),
        (H, Z - 1),
        (H, R - 1),
        (),
        (R - 1,),
        (Z - 1,),
        (Z - 1,),
        (R - 1,),
        (),
    ):
        scratch += [dma(shape), dma(shape)]
    whole = pl.BlockSpec(memory_space=pltpu.VMEM)
    scalars = pl.BlockSpec(memory_space=pltpu.SMEM)
    node_out, weight_grad, feature_grad = pl.pallas_call(
        functools.partial(kernel, R, C, scale),
        out_shape=(
            jax.ShapeDtypeStruct((T, F), BF),
            jax.ShapeDtypeStruct((F, F), BF),
            jax.ShapeDtypeStruct((T, F), BF),
        ),
        in_specs=[scalars] * 3 + [pl.BlockSpec(memory_space=pl.ANY)] + [whole] * 3,
        out_specs=(whole, whole, whole),
        scratch_shapes=scratch,
        compiler_params=pltpu.CompilerParams(
            collective_id=0, has_side_effects=True, vmem_limit_bytes=60 * 1024 * 1024
        ),
        name="layer",
    )(tile_rows, tile_cols, tile_counts, adj_tiles, features, weight, node_grad)
    return pl.pallas_call(
        hand_over,
        out_shape=(
            jax.ShapeDtypeStruct((T, F), BF),
            jax.ShapeDtypeStruct((F, F), F32),
            jax.ShapeDtypeStruct((T, F), BF),
        ),
        in_specs=[whole] * 3,
        out_specs=(whole, whole, whole),
        name="hand_over",
    )(node_out, weight_grad, feature_grad)


def solution(mesh):
    in_specs = (
        P("row", "col", None, None, None),
        P("row", "col", None),
        P("row", "col", None),
        P("row", "col"),
        P(("col", "row"), None),
        P(),
        P(("row", "col"), None),
    )
    out_specs = (P(("row", "col"), None), P(), P(("col", "row"), None))
    return jax.shard_map(local, mesh=mesh, in_specs=in_specs, out_specs=out_specs, check_vma=False)
```

```python
import functools

import jax
import jax.numpy as jnp
from jax import lax
from jax.experimental import pallas as pl
from jax.experimental.pallas import tpu as pltpu
from jax.sharding import PartitionSpec as P

BF = jnp.bfloat16
F32 = jnp.float32
CHUNKS = 4


def dot(a, b):
    return jnp.dot(a, b, preferred_element_type=F32)


def kernel(
    R,
    C,
    scale,
    rows_s,
    cols_s,
    count_s,
    adj_hbm,
    feat,
    weight,
    ngrad,
    out,
    wfull,
    fgrad,
    adj,
    dense,
    feats,
    chip,
    sib_send,
    sib_recv,
    up_recv,
    dn_recv,
    agg,
    dpre_v,
    grads,
    b_send,
    b_recv,
    wterm,
    w0_send,
    w0_recv,
    w_pair,
    w1_send,
    w1_recv,
    w1_sum,
    w2_send,
    w2_recv,
    wslab,
    adj_sem,
    f_s,
    f_r,
    sib_s,
    sib_r,
    up_s,
    up_r,
    dn_s,
    dn_r,
    gsib_s,
    gsib_r,
    gup_s,
    gup_r,
    gdn_s,
    gdn_r,
    b_s,
    b_r,
    w0_s,
    w0_r,
    w1_s,
    w1_r,
    w2_s,
    w2_r,
    w3_s,
    w3_r,
    w4_s,
    w4_r,
    w5_s,
    w5_r,
):
    H = CHUNKS
    Z = C // 2
    T, F = feat.shape
    W = F // H
    slots = adj.shape[0] - 1
    i = lax.axis_index("row")
    j = lax.axis_index("col")
    z = j // 2
    c = lax.rem(j, 2)
    sibling = 2 * z + 1 - c
    pending = []

    def remote(src, dst, ssem, rsem, row, col):
        return pltpu.make_async_remote_copy(
            src_ref=src,
            dst_ref=dst,
            send_sem=ssem,
            recv_sem=rsem,
            device_id=(row, col),
            device_id_type=pl.DeviceIdType.MESH,
        )

    def send(copy, cond=None):
        if cond is None:
            copy.start()
        else:
            pl.when(cond)(copy.start)
        pending.append((copy, cond))

    adj_copy = pltpu.make_async_copy(adj_hbm.at[0, 0], adj.at[pl.ds(0, slots)], adj_sem)
    adj_copy.start()

    barrier = pltpu.get_barrier_semaphore()
    for q in range(1, R):
        pl.semaphore_signal(
            barrier, inc=1, device_id=(lax.rem(i + q, R), j), device_id_type=pl.DeviceIdType.MESH
        )
    for q in range(1, Z):
        pl.semaphore_signal(
            barrier,
            inc=1,
            device_id=(i, 2 * lax.rem(z + q, Z) + c),
            device_id_type=pl.DeviceIdType.MESH,
        )
    pl.semaphore_signal(
        barrier, inc=1, device_id=(i, sibling), device_id_type=pl.DeviceIdType.MESH
    )
    pl.semaphore_wait(barrier, R + Z - 1)

    def tile_at(index):
        return pl.ds(pl.multiple_of(index * T, T), T)

    def feat_copy(h, q):
        return remote(
            feat.at[:, pl.ds(h * W, W)],
            feats.at[h, tile_at(i), :],
            f_s.at[h, q - 1],
            f_r.at[h, q - 1],
            lax.rem(i + q, R),
            j,
        )

    for h in range(H):
        for q in range(1, R):
            send(feat_copy(h, q))
    for h in range(H):
        feats[h, tile_at(i), :] = feat[:, pl.ds(h * W, W)]

    adj[slots] = jnp.zeros((T, T), BF)
    adj_copy.wait()
    count = count_s[0, 0]

    def fill(r, carry):
        for k in range(R):
            found = jnp.int32(slots)
            for t in range(slots):
                hit = (rows_s[0, 0, t] == r) & (cols_s[0, 0, t] == k) & (t < count)
                found = jnp.where(hit, jnp.int32(t), found)
            dense[tile_at(lax.rem(r, 2) * Z + r // 2), k * T : (k + 1) * T] = adj[found]
        return carry

    lax.fori_loop(0, C, fill, 0)

    def core_rows(core):
        return pl.ds(pl.multiple_of(core * Z * T, Z * T), Z * T)

    def sib_copy(h):
        return remote(sib_send.at[h], sib_recv.at[h], sib_s.at[h], sib_r.at[h], i, sibling)

    def forward(h):
        for q in range(1, R):
            feat_copy(h, q).wait_recv()
        sib_send[h] = dot(dense[core_rows(1 - c), :], feats[h]).astype(BF)
        send(sib_copy(h))
        part = dot(dense[core_rows(c), :], feats[h])
        sib_copy(h).wait_recv()
        chip[h] = (part + sib_recv[h].astype(F32)).astype(BF)

    above = jnp.minimum(z + 1, Z - 1)
    below = jnp.maximum(z - 1, 0)

    def up_copy(h, s):
        return remote(
            chip.at[h, pl.ds((Z - 1 - s) * T, T)], up_recv.at[h, s], up_s.at[h, s], up_r.at[h, s], i, 2 * above + c
        )

    def dn_copy(h, s):
        return remote(
            chip.at[h, pl.ds(s * T, T)], dn_recv.at[h, s], dn_s.at[h, s], dn_r.at[h, s], i, 2 * below + c
        )

    def chain(h, s):
        d = Z - 1 - s

        @pl.when((z > 0) & (z < d))
        def _():
            up_copy(h, s).wait_recv()
            chip[h, d * T : (d + 1) * T] = (chip[h, d * T : (d + 1) * T].astype(F32) + up_recv[h, s].astype(F32)).astype(BF)

        send(up_copy(h, s), z < d)

        @pl.when((z < Z - 1) & (z > s))
        def _():
            dn_copy(h, s).wait_recv()
            chip[h, s * T : (s + 1) * T] = (chip[h, s * T : (s + 1) * T].astype(F32) + dn_recv[h, s].astype(F32)).astype(BF)

        send(dn_copy(h, s), z > s)

    def finish(h):
        cols = pl.ds(h * W, W)

        @pl.when(z == 0)
        def _():
            dn_copy(h, z).wait_recv()
            agg[:, cols] = (chip[h, tile_at(z)].astype(F32) + dn_recv[h, z].astype(F32)).astype(BF)

        @pl.when(z == Z - 1)
        def _():
            up_copy(h, Z - 1 - z).wait_recv()
            agg[:, cols] = (chip[h, tile_at(z)].astype(F32) + up_recv[h, Z - 1 - z].astype(F32)).astype(BF)

        @pl.when((z > 0) & (z < Z - 1))
        def _():
            up_copy(h, Z - 1 - z).wait_recv()
            dn_copy(h, z).wait_recv()
            both = up_recv[h, Z - 1 - z].astype(F32) + dn_recv[h, z].astype(F32)
            agg[:, cols] = (chip[h, tile_at(z)].astype(F32) + both).astype(BF)

    for wave in range(H + Z - 2):
        for s in range(Z - 2, 0, -1):
            if 0 <= wave - s < H:
                chain(wave - s, s)
        if wave < H:
            forward(wave)
            chain(wave, 0)
    for h in range(H):
        finish(h)

    pre = dot(agg[...], weight[...])
    sigma = 1.0 / (1.0 + jnp.exp(-pre))
    dpre = (ngrad[...].astype(F32) * sigma * (1.0 + pre * (1.0 - sigma))).astype(BF)
    dpre_v[...] = dpre

    def gsib_copy(h, owner):
        r = c * Z + owner
        return remote(
            grads.at[h, :, tile_at(r)], grads.at[h, :, tile_at(r)], gsib_s.at[h, owner], gsib_r.at[h, owner],
            i, sibling,
        )

    def gup_copy(h, s):
        r = c * Z + jnp.maximum(z - s, 0)
        return remote(
            grads.at[h, :, tile_at(r)], grads.at[h, :, tile_at(r)], gup_s.at[h, s], gup_r.at[h, s],
            i, 2 * above + c,
        )

    def gdn_copy(h, s):
        r = c * Z + jnp.minimum(z + s, Z - 1)
        return remote(
            grads.at[h, :, tile_at(r)], grads.at[h, :, tile_at(r)], gdn_s.at[h, s], gdn_r.at[h, s],
            i, 2 * below + c,
        )

    turned = lax.dot_general(
        weight[...], dpre_v[...], (((1,), (1,)), ((), ())), preferred_element_type=F32
    ).astype(BF)
    for h in range(H):
        grads[h, :, tile_at(c * Z + z)] = turned[h * W : (h + 1) * W, :]

    def give(h):
        send(gup_copy(h, 0), z < Z - 1)
        send(gdn_copy(h, 0), z > 0)
        send(gsib_copy(h, z))

    give(0)
    give(1)
    out[...] = (pre * sigma).astype(BF)

    half = F // 2
    S1 = half // R
    groups = S1 // 16
    cg = Z // groups
    width = F // cg

    def slab_at(index):
        return pl.ds(pl.multiple_of(index * S1, S1), S1)

    def half_at(index):
        return pl.ds(pl.multiple_of(index * half, half), half)

    def piece_at(index):
        return (
            pl.ds(pl.multiple_of(index // cg * 16, 16), 16),
            pl.ds(pl.multiple_of(lax.rem(index, cg) * width, width), width),
        )

    w0_copy = remote(w0_send, w0_recv, w0_s, w0_r, i, sibling)

    def w1_copy(q):
        return remote(
            w1_send.at[q - 1], w1_recv.at[q - 1], w1_s.at[q - 1], w1_r.at[q - 1],
            lax.rem(i + q, R), j,
        )

    def w2_copy(q):
        return remote(
            w2_send.at[q - 1], w2_recv.at[q - 1], w2_s.at[q - 1], w2_r.at[q - 1],
            i, 2 * lax.rem(z + q, Z) + c,
        )

    def w3_copy(q, owner):
        r, k = piece_at(owner)
        return remote(
            wslab.at[r, k], wslab.at[r, k], w3_s.at[q - 1], w3_r.at[q - 1],
            i, 2 * lax.rem(z + q, Z) + c,
        )

    def w4_copy(q, owner):
        rows = slab_at(c * R + owner)
        return remote(
            wslab, wfull.at[rows, :], w4_s.at[q - 1], w4_r.at[q - 1], lax.rem(i + q, R), j
        )

    def w5_copy(core):
        rows = half_at(core)
        return remote(wfull.at[rows, :], wfull.at[rows, :], w5_s, w5_r, i, sibling)

    wterm[...] = (
        lax.dot_general(
            agg[...], dpre_v[...], (((0,), (0,)), ((), ())), preferred_element_type=F32
        )
        * scale
    )
    w0_send[...] = wterm[half_at(1 - c), :].astype(BF)
    send(w0_copy)

    def sum_pair():
        w0_copy.wait_recv()
        w_pair[...] = wterm[half_at(c), :] + w0_recv[...].astype(F32)
        for q in range(1, R):
            w1_send[q - 1] = w_pair[slab_at(lax.rem(i + q, R)), :].astype(BF)
            send(w1_copy(q))

    def sum_row():
        acc = w_pair[slab_at(i), :]
        for q in range(1, R):
            w1_copy(q).wait_recv()
            acc = acc + w1_recv[q - 1].astype(F32)
        w1_sum[...] = acc
        for q in range(1, Z):
            r, k = piece_at(lax.rem(z + q, Z))
            w2_send[q - 1] = w1_sum[r, k].astype(BF)
            send(w2_copy(q))

    def sum_chain():
        r, k = piece_at(z)
        acc = w1_sum[r, k]
        for q in range(1, Z):
            w2_copy(q).wait_recv()
            acc = acc + w2_recv[q - 1].astype(F32)
        wslab[r, k] = acc.astype(BF)
        for q in range(1, Z):
            send(w3_copy(q, z))

    def share_row():
        for q in range(1, Z):
            w3_copy(q, lax.rem(z - q + Z, Z)).wait_recv()
        for q in range(1, R):
            send(w4_copy(q, i))
        wfull[slab_at(c * R + i), :] = wslab[...]

    def share_pair():
        for q in range(1, R):
            w4_copy(q, lax.rem(i - q + R, R)).wait_recv()
        send(w5_copy(c))

    def gather(h, s):
        from_below = z - 1 - s >= 0
        from_above = z + 1 + s <= Z - 1

        @pl.when(from_below)
        def _():
            gup_copy(h, s).wait_recv()

        if s + 1 < Z - 1:
            send(gup_copy(h, s + 1), from_below & (z < Z - 1))
        send(gsib_copy(h, jnp.maximum(z - 1 - s, 0)), from_below)

        @pl.when(from_above)
        def _():
            gdn_copy(h, s).wait_recv()

        if s + 1 < Z - 1:
            send(gdn_copy(h, s + 1), from_above & (z > 0))
        send(gsib_copy(h, jnp.minimum(z + 1 + s, Z - 1)), from_above)

    def b_copy(h, q):
        return remote(
            b_send.at[h, q - 1], b_recv.at[h, q - 1], b_s.at[h, q - 1], b_r.at[h, q - 1],
            lax.rem(i + q, R), j,
        )

    def cell_cols(h, k):
        return dot(grads[h], dense[:, tile_at(k)])

    def backward(h):
        for d in range(Z):
            gsib_copy(h, d).wait_recv()
        for q in range(1, R):
            b_send[h, q - 1] = cell_cols(h, lax.rem(i + q, R)).astype(BF)
            send(b_copy(h, q))

    def total(h):
        acc = cell_cols(h, i)
        for q in range(1, R):
            b_copy(h, q).wait_recv()
            acc = acc + b_recv[h, q - 1].astype(F32)
        fgrad[:, h * W : (h + 1) * W] = acc.T.astype(BF)

    for wave in range(H + Z - 2):
        for s in range(Z - 2, -1, -1):
            if 0 <= wave - s < H:
                gather(wave - s, s)
        if wave + 2 < H:
            give(wave + 2)
        if wave == 0:
            sum_pair()
        if wave == 1:
            sum_row()
        h = wave - (Z - 2)
        if h >= 0:
            backward(h)
            if h == 0:
                sum_chain()
            if h == 1:
                share_row()
            if h == 2:
                share_pair()
            if h >= 1:
                total(h - 1)
    total(H - 1)
    w5_copy(1 - c).wait_recv()

    for copy, cond in pending:
        if cond is None:
            copy.wait_send()
        else:
            pl.when(cond)(copy.wait_send)


def hand_over(node_in, weight_in, feature_in, node_out, weight_out, feature_out):
    node_out[...] = node_in[...]
    weight_out[...] = weight_in[...].astype(F32)
    feature_out[...] = feature_in[...]


def local(adj_tiles, tile_rows, tile_cols, tile_counts, features, weight, node_grad):
    R = lax.axis_size("row")
    C = lax.axis_size("col")
    Z = C // 2
    H = CHUNKS
    T, F = features.shape
    W = F // H
    slots = adj_tiles.shape[2]
    S1 = F // 2 // R
    width = F // (Z // (S1 // 16))
    scale = float((T * R * C) ** -0.5)
    vmem = pltpu.VMEM
    dma = pltpu.SemaphoreType.DMA
    scratch = [
        vmem((slots + 1, T, T), BF),
        vmem((C * T, R * T), BF),
        vmem((H, R * T, W), BF),
        vmem((H, Z * T, W), BF),
        vmem((H, Z * T, W), BF),
        vmem((H, Z * T, W), BF),
        vmem((H, Z - 1, T, W), BF),
        vmem((H, Z - 1, T, W), BF),
        vmem((T, F), BF),
        vmem((T, F), BF),
        vmem((H, W, C * T), BF),
        vmem((H, R - 1, W, T), BF),
        vmem((H, R - 1, W, T), BF),
        vmem((F, F), F32),
        vmem((F // 2, F), BF),
        vmem((F // 2, F), BF),
        vmem((F // 2, F), F32),
        vmem((R - 1, S1, F), BF),
        vmem((R - 1, S1, F), BF),
        vmem((S1, F), F32),
        vmem((Z - 1, 16, width), BF),
        vmem((Z - 1, 16, width), BF),
        vmem((S1, F), BF),
        dma(()),
    ]
    for shape in (
        (H, R - 1),
        (H,),
        (H, Z - 1),
        (H, Z - 1),
        (H, Z),
        (H, Z - 1),
        (H, Z - 1),
        (H, R - 1),
        (),
        (R - 1,),
        (Z - 1,),
        (Z - 1,),
        (R - 1,),
        (),
    ):
        scratch += [dma(shape), dma(shape)]
    whole = pl.BlockSpec(memory_space=pltpu.VMEM)
    scalars = pl.BlockSpec(memory_space=pltpu.SMEM)
    node_out, weight_grad, feature_grad = pl.pallas_call(
        functools.partial(kernel, R, C, scale),
        out_shape=(
            jax.ShapeDtypeStruct((T, F), BF),
            jax.ShapeDtypeStruct((F, F), BF),
            jax.ShapeDtypeStruct((T, F), BF),
        ),
        in_specs=[scalars] * 3 + [pl.BlockSpec(memory_space=pl.ANY)] + [whole] * 3,
        out_specs=(whole, whole, whole),
        scratch_shapes=scratch,
        compiler_params=pltpu.CompilerParams(
            collective_id=0, has_side_effects=True, vmem_limit_bytes=60 * 1024 * 1024
        ),
        name="layer",
    )(tile_rows, tile_cols, tile_counts, adj_tiles, features, weight, node_grad)
    return pl.pallas_call(
        hand_over,
        out_shape=(
            jax.ShapeDtypeStruct((T, F), BF),
            jax.ShapeDtypeStruct((F, F), F32),
            jax.ShapeDtypeStruct((T, F), BF),
        ),
        in_specs=[whole] * 3,
        out_specs=(whole, whole, whole),
        name="hand_over",
    )(node_out, weight_grad, feature_grad)


def solution(mesh):
    in_specs = (
        P("row", "col", None, None, None),
        P("row", "col", None),
        P("row", "col", None),
        P("row", "col"),
        P(("col", "row"), None),
        P(),
        P(("row", "col"), None),
    )
    out_specs = (P(("row", "col"), None), P(), P(("col", "row"), None))
    return jax.shard_map(local, mesh=mesh, in_specs=in_specs, out_specs=out_specs, check_vma=False)
```

```python
import functools

import jax
import jax.numpy as jnp
from jax import lax
from jax.experimental import pallas as pl
from jax.experimental.pallas import tpu as pltpu
from jax.sharding import PartitionSpec as P

BF = jnp.bfloat16
F32 = jnp.float32
CHUNKS = 2


def dot(a, b):
    return jnp.dot(a, b, preferred_element_type=F32)


def kernel(
    R,
    C,
    scale,
    rows_s,
    cols_s,
    count_s,
    adj_hbm,
    feat,
    weight,
    ngrad,
    out,
    wfull,
    fgrad,
    adj,
    dense,
    feats,
    chip,
    sib_send,
    sib_recv,
    up_recv,
    dn_recv,
    agg,
    dpre_v,
    grads,
    wide,
    b_own,
    b_send,
    b_recv,
    wterm,
    w0_send,
    w0_recv,
    w_pair,
    w1_send,
    w1_recv,
    w1_sum,
    w2_send,
    w2_recv,
    wslab,
    adj_sem,
    f_s,
    f_r,
    sib_s,
    sib_r,
    up_s,
    up_r,
    dn_s,
    dn_r,
    gsib_s,
    gsib_r,
    gup_s,
    gup_r,
    gdn_s,
    gdn_r,
    b_s,
    b_r,
    w0_s,
    w0_r,
    w1_s,
    w1_r,
    w2_s,
    w2_r,
    w3_s,
    w3_r,
    w4_s,
    w4_r,
    w5_s,
    w5_r,
):
    H = CHUNKS
    Z = C // 2
    T, F = feat.shape
    W = F // H
    slots = adj.shape[0] - 1
    i = lax.axis_index("row")
    j = lax.axis_index("col")
    z = j // 2
    c = lax.rem(j, 2)
    sibling = 2 * z + 1 - c
    pending = []

    def remote(src, dst, ssem, rsem, row, col):
        return pltpu.make_async_remote_copy(
            src_ref=src,
            dst_ref=dst,
            send_sem=ssem,
            recv_sem=rsem,
            device_id=(row, col),
            device_id_type=pl.DeviceIdType.MESH,
        )

    def send(copy, cond=None):
        if cond is None:
            copy.start()
        else:
            pl.when(cond)(copy.start)
        pending.append((copy, cond))

    adj_copy = pltpu.make_async_copy(adj_hbm.at[0, 0], adj.at[pl.ds(0, slots)], adj_sem)
    adj_copy.start()

    def tile_at(index):
        return pl.ds(pl.multiple_of(index * T, T), T)

    for h in range(H):
        feats[h, tile_at(i), :] = feat[:, pl.ds(h * W, W)]
    barrier = pltpu.get_barrier_semaphore()
    for q in range(1, R):
        pl.semaphore_signal(
            barrier, inc=1, device_id=(lax.rem(i + q, R), j), device_id_type=pl.DeviceIdType.MESH
        )
    for q in range(1, Z):
        pl.semaphore_signal(
            barrier,
            inc=1,
            device_id=(i, 2 * lax.rem(z + q, Z) + c),
            device_id_type=pl.DeviceIdType.MESH,
        )
    pl.semaphore_signal(
        barrier, inc=1, device_id=(i, sibling), device_id_type=pl.DeviceIdType.MESH
    )
    pl.semaphore_wait(barrier, R + Z - 1)

    def feat_copy(h, q):
        return remote(
            feats.at[h, tile_at(i), :],
            feats.at[h, tile_at(i), :],
            f_s.at[h, q - 1],
            f_r.at[h, q - 1],
            lax.rem(i + q, R),
            j,
        )

    for h in range(H):
        for q in range(1, R):
            send(feat_copy(h, q))

    adj[slots] = jnp.zeros((T, T), BF)
    adj_copy.wait()
    count = count_s[0, 0]

    def fill(r, carry):
        for k in range(R):
            found = jnp.int32(slots)
            for t in range(slots):
                hit = (rows_s[0, 0, t] == r) & (cols_s[0, 0, t] == k) & (t < count)
                found = jnp.where(hit, jnp.int32(t), found)
            dense[tile_at(lax.rem(r, 2) * Z + r // 2), k * T : (k + 1) * T] = adj[found]
        return carry

    lax.fori_loop(0, C, fill, 0)

    step = min(Z, 4) * T

    def core_rows(core, first):
        return pl.ds(pl.multiple_of(core * Z * T + first, step), step)

    def sib_copy(h):
        return remote(sib_send.at[h], sib_recv.at[h], sib_s.at[h], sib_r.at[h], i, sibling)

    def forward(h):
        for q in range(1, R):
            feat_copy(h, q).wait_recv()
        for first in range(0, Z * T, step):
            part = dot(dense[core_rows(1 - c, first), :], feats[h])
            sib_send[h, first : first + step] = part.astype(BF)
        send(sib_copy(h))
        for first in range(0, Z * T, step):
            part = dot(dense[core_rows(c, first), :], feats[h])
            if first == 0:
                sib_copy(h).wait_recv()
            part = part + sib_recv[h, first : first + step].astype(F32)
            chip[h, first : first + step] = part.astype(BF)

    above = jnp.minimum(z + 1, Z - 1)
    below = jnp.maximum(z - 1, 0)

    def up_copy(h, s):
        return remote(
            chip.at[h, pl.ds((Z - 1 - s) * T, T)], up_recv.at[h, s], up_s.at[h, s], up_r.at[h, s], i, 2 * above + c
        )

    def dn_copy(h, s):
        return remote(
            chip.at[h, pl.ds(s * T, T)], dn_recv.at[h, s], dn_s.at[h, s], dn_r.at[h, s], i, 2 * below + c
        )

    def chain(h, s):
        d = Z - 1 - s

        @pl.when((z > 0) & (z < d))
        def _():
            up_copy(h, s).wait_recv()
            chip[h, d * T : (d + 1) * T] = (chip[h, d * T : (d + 1) * T].astype(F32) + up_recv[h, s].astype(F32)).astype(BF)

        send(up_copy(h, s), z < d)

        @pl.when((z < Z - 1) & (z > s))
        def _():
            dn_copy(h, s).wait_recv()
            chip[h, s * T : (s + 1) * T] = (chip[h, s * T : (s + 1) * T].astype(F32) + dn_recv[h, s].astype(F32)).astype(BF)

        send(dn_copy(h, s), z > s)

    def finish(h):
        cols = pl.ds(h * W, W)

        @pl.when(z == 0)
        def _():
            dn_copy(h, z).wait_recv()
            agg[:, cols] = (chip[h, tile_at(z)].astype(F32) + dn_recv[h, z].astype(F32)).astype(BF)

        @pl.when(z == Z - 1)
        def _():
            up_copy(h, Z - 1 - z).wait_recv()
            agg[:, cols] = (chip[h, tile_at(z)].astype(F32) + up_recv[h, Z - 1 - z].astype(F32)).astype(BF)

        @pl.when((z > 0) & (z < Z - 1))
        def _():
            up_copy(h, Z - 1 - z).wait_recv()
            dn_copy(h, z).wait_recv()
            both = up_recv[h, Z - 1 - z].astype(F32) + dn_recv[h, z].astype(F32)
            agg[:, cols] = (chip[h, tile_at(z)].astype(F32) + both).astype(BF)

    for wave in range(H + Z - 2):
        for s in range(Z - 2, 0, -1):
            if 0 <= wave - s < H:
                chain(wave - s, s)
        if wave < H:
            forward(wave)
            chain(wave, 0)
    for h in range(H):
        finish(h)

    pre = dot(agg[...], weight[...])
    sigma = 1.0 / (1.0 + jnp.exp(-pre))
    dpre = (ngrad[...].astype(F32) * sigma * (1.0 + pre * (1.0 - sigma))).astype(BF)
    dpre_v[...] = dpre

    def gsib_copy(h, owner):
        r = c * Z + owner
        return remote(
            grads.at[h, r], grads.at[h, r], gsib_s.at[h, owner], gsib_r.at[h, owner],
            i, sibling,
        )

    def gup_copy(h, s):
        r = c * Z + jnp.maximum(z - s, 0)
        return remote(
            grads.at[h, r], grads.at[h, r], gup_s.at[h, s], gup_r.at[h, s],
            i, 2 * above + c,
        )

    def gdn_copy(h, s):
        r = c * Z + jnp.minimum(z + s, Z - 1)
        return remote(
            grads.at[h, r], grads.at[h, r], gdn_s.at[h, s], gdn_r.at[h, s],
            i, 2 * below + c,
        )

    turned = lax.dot_general(
        weight[...], dpre_v[...], (((1,), (1,)), ((), ())), preferred_element_type=F32
    ).astype(BF)
    for h in range(H):
        grads[h, c * Z + z] = turned[h * W : (h + 1) * W, :]

    def give(h):
        send(gup_copy(h, 0), z < Z - 1)
        send(gdn_copy(h, 0), z > 0)
        send(gsib_copy(h, z))

    give(0)
    give(1)
    out[...] = (pre * sigma).astype(BF)

    half = F // 2
    S1 = half // R
    groups = S1 // 16
    cg = Z // groups
    width = F // cg

    def slab_at(index):
        return pl.ds(pl.multiple_of(index * S1, S1), S1)

    def half_at(index):
        return pl.ds(pl.multiple_of(index * half, half), half)

    def piece_at(index):
        return (
            pl.ds(pl.multiple_of(index // cg * 16, 16), 16),
            pl.ds(pl.multiple_of(lax.rem(index, cg) * width, width), width),
        )

    w0_copy = remote(w0_send, w0_recv, w0_s, w0_r, i, sibling)

    def w1_copy(q):
        return remote(
            w1_send.at[q - 1], w1_recv.at[q - 1], w1_s.at[q - 1], w1_r.at[q - 1],
            lax.rem(i + q, R), j,
        )

    def w2_copy(q):
        return remote(
            w2_send.at[q - 1], w2_recv.at[q - 1], w2_s.at[q - 1], w2_r.at[q - 1],
            i, 2 * lax.rem(z + q, Z) + c,
        )

    def w3_copy(q, owner):
        r, k = piece_at(owner)
        return remote(
            wslab.at[r, k], wslab.at[r, k], w3_s.at[q - 1], w3_r.at[q - 1],
            i, 2 * lax.rem(z + q, Z) + c,
        )

    def w4_copy(q, owner):
        rows = slab_at(c * R + owner)
        return remote(
            wslab, wfull.at[rows, :], w4_s.at[q - 1], w4_r.at[q - 1], lax.rem(i + q, R), j
        )

    def w5_copy(core):
        rows = half_at(core)
        return remote(wfull.at[rows, :], wfull.at[rows, :], w5_s, w5_r, i, sibling)

    wterm[...] = (
        lax.dot_general(
            agg[...], dpre_v[...], (((0,), (0,)), ((), ())), preferred_element_type=F32
        )
        * scale
    )
    w0_send[...] = wterm[half_at(1 - c), :].astype(BF)
    send(w0_copy)

    def sum_pair():
        w0_copy.wait_recv()
        w_pair[...] = wterm[half_at(c), :] + w0_recv[...].astype(F32)
        for q in range(1, R):
            w1_send[q - 1] = w_pair[slab_at(lax.rem(i + q, R)), :].astype(BF)
            send(w1_copy(q))

    def sum_row():
        acc = w_pair[slab_at(i), :]
        for q in range(1, R):
            w1_copy(q).wait_recv()
            acc = acc + w1_recv[q - 1].astype(F32)
        w1_sum[...] = acc
        for q in range(1, Z):
            r, k = piece_at(lax.rem(z + q, Z))
            w2_send[q - 1] = w1_sum[r, k].astype(BF)
            send(w2_copy(q))

    def sum_chain():
        r, k = piece_at(z)
        acc = w1_sum[r, k]
        for q in range(1, Z):
            w2_copy(q).wait_recv()
            acc = acc + w2_recv[q - 1].astype(F32)
        wslab[r, k] = acc.astype(BF)
        for q in range(1, Z):
            send(w3_copy(q, z))

    def share_row():
        for q in range(1, Z):
            w3_copy(q, lax.rem(z - q + Z, Z)).wait_recv()
        for q in range(1, R):
            send(w4_copy(q, i))
        wfull[slab_at(c * R + i), :] = wslab[...]

    def share_pair():
        for q in range(1, R):
            w4_copy(q, lax.rem(i - q + R, R)).wait_recv()
        send(w5_copy(c))

    def gather(h, s):
        from_below = z - 1 - s >= 0
        from_above = z + 1 + s <= Z - 1

        @pl.when(from_below)
        def _():
            gup_copy(h, s).wait_recv()

        if s + 1 < Z - 1:
            send(gup_copy(h, s + 1), from_below & (z < Z - 1))
        send(gsib_copy(h, jnp.maximum(z - 1 - s, 0)), from_below)

        @pl.when(from_above)
        def _():
            gdn_copy(h, s).wait_recv()

        if s + 1 < Z - 1:
            send(gdn_copy(h, s + 1), from_above & (z > 0))
        send(gsib_copy(h, jnp.minimum(z + 1 + s, Z - 1)), from_above)

    def b_copy(h, q):
        return remote(
            b_send.at[h, q - 1], b_recv.at[h, q - 1], b_s.at[h, q - 1], b_r.at[h, q - 1],
            lax.rem(i + q, R), j,
        )

    def cell_cols(k):
        return dot(wide[...], dense[:, tile_at(k)])

    def backward(h):
        for d in range(Z):
            gsib_copy(h, d).wait_recv()
        for r in range(C):
            wide[:, r * T : (r + 1) * T] = grads[h, r]
        for q in range(1, R):
            b_send[h, q - 1] = cell_cols(lax.rem(i + q, R)).astype(BF)
            send(b_copy(h, q))
        b_own[h] = cell_cols(i)

    def total(h):
        acc = b_own[h]
        for q in range(1, R):
            b_copy(h, q).wait_recv()
            acc = acc + b_recv[h, q - 1].astype(F32)
        fgrad[:, h * W : (h + 1) * W] = acc.T.astype(BF)

    for wave in range(H + Z - 2):
        for s in range(Z - 2, -1, -1):
            if 0 <= wave - s < H:
                gather(wave - s, s)
        if wave + 2 < H:
            give(wave + 2)
        if wave == 0:
            sum_pair()
        if wave == 1:
            sum_row()
        h = wave - (Z - 2)
        if h == H - 1:
            share_row()
        if h >= 0:
            backward(h)
        if h == 0:
            sum_chain()
    for h in range(H - 1):
        total(h)
    share_pair()
    total(H - 1)
    w5_copy(1 - c).wait_recv()

    for copy, cond in pending:
        if cond is None:
            copy.wait_send()
        else:
            pl.when(cond)(copy.wait_send)


def hand_over(node_in, weight_in, feature_in, node_out, weight_out, feature_out):
    node_out[...] = node_in[...]
    weight_out[...] = weight_in[...].astype(F32)
    feature_out[...] = feature_in[...]


def local(adj_tiles, tile_rows, tile_cols, tile_counts, features, weight, node_grad):
    R = lax.axis_size("row")
    C = lax.axis_size("col")
    Z = C // 2
    H = CHUNKS
    T, F = features.shape
    W = F // H
    slots = adj_tiles.shape[2]
    S1 = F // 2 // R
    width = F // (Z // (S1 // 16))
    scale = float((T * R * C) ** -0.5)
    vmem = pltpu.VMEM
    dma = pltpu.SemaphoreType.DMA
    scratch = [
        vmem((slots + 1, T, T), BF),
        vmem((C * T, R * T), BF),
        vmem((H, R * T, W), BF),
        vmem((H, Z * T, W), BF),
        vmem((H, Z * T, W), BF),
        vmem((H, Z * T, W), BF),
        vmem((H, Z - 1, T, W), BF),
        vmem((H, Z - 1, T, W), BF),
        vmem((T, F), BF),
        vmem((T, F), BF),
        vmem((H, C, W, T), BF),
        vmem((W, C * T), BF),
        vmem((H, W, T), F32),
        vmem((H, R - 1, W, T), BF),
        vmem((H, R - 1, W, T), BF),
        vmem((F, F), F32),
        vmem((F // 2, F), BF),
        vmem((F // 2, F), BF),
        vmem((F // 2, F), F32),
        vmem((R - 1, S1, F), BF),
        vmem((R - 1, S1, F), BF),
        vmem((S1, F), F32),
        vmem((Z - 1, 16, width), BF),
        vmem((Z - 1, 16, width), BF),
        vmem((S1, F), BF),
        dma(()),
    ]
    for shape in (
        (H, R - 1),
        (H,),
        (H, Z - 1),
        (H, Z - 1),
        (H, Z),
        (H, Z - 1),
        (H, Z - 1),
        (H, R - 1),
        (),
        (R - 1,),
        (Z - 1,),
        (Z - 1,),
        (R - 1,),
        (),
    ):
        scratch += [dma(shape), dma(shape)]
    whole = pl.BlockSpec(memory_space=pltpu.VMEM)
    scalars = pl.BlockSpec(memory_space=pltpu.SMEM)
    node_out, weight_grad, feature_grad = pl.pallas_call(
        functools.partial(kernel, R, C, scale),
        out_shape=(
            jax.ShapeDtypeStruct((T, F), BF),
            jax.ShapeDtypeStruct((F, F), BF),
            jax.ShapeDtypeStruct((T, F), BF),
        ),
        in_specs=[scalars] * 3 + [pl.BlockSpec(memory_space=pl.ANY)] + [whole] * 3,
        out_specs=(whole, whole, whole),
        scratch_shapes=scratch,
        compiler_params=pltpu.CompilerParams(
            collective_id=0, has_side_effects=True, vmem_limit_bytes=62 * 1024 * 1024
        ),
        name="layer",
    )(tile_rows, tile_cols, tile_counts, adj_tiles, features, weight, node_grad)
    return pl.pallas_call(
        hand_over,
        out_shape=(
            jax.ShapeDtypeStruct((T, F), BF),
            jax.ShapeDtypeStruct((F, F), F32),
            jax.ShapeDtypeStruct((T, F), BF),
        ),
        in_specs=[whole] * 3,
        out_specs=(whole, whole, whole),
        name="hand_over",
    )(node_out, weight_grad, feature_grad)


def solution(mesh):
    in_specs = (
        P("row", "col", None, None, None),
        P("row", "col", None),
        P("row", "col", None),
        P("row", "col"),
        P(("col", "row"), None),
        P(),
        P(("row", "col"), None),
    )
    out_specs = (P(("row", "col"), None), P(), P(("col", "row"), None))
    return jax.shard_map(local, mesh=mesh, in_specs=in_specs, out_specs=out_specs, check_vma=False)
```

```python
import functools

import jax
import jax.numpy as jnp
from jax import lax
from jax.experimental import pallas as pl
from jax.experimental.pallas import tpu as pltpu
from jax.sharding import PartitionSpec as P

BF = jnp.bfloat16
F32 = jnp.float32
CHUNKS = 2


def dot(a, b):
    return jnp.dot(a, b, preferred_element_type=F32)


def kernel(
    R,
    C,
    scale,
    rows_s,
    cols_s,
    count_s,
    adj_hbm,
    feat,
    weight,
    ngrad,
    out,
    wfull,
    fgrad,
    adj,
    dense,
    feats,
    chip,
    sib_send,
    sib_recv,
    up_recv,
    dn_recv,
    agg,
    dpre_v,
    grads,
    wide,
    b_own,
    b_send,
    b_recv,
    wterm,
    w0_send,
    w0_recv,
    w_pair,
    w1_send,
    w1_recv,
    w1_sum,
    w2_send,
    w2_recv,
    wslab,
    adj_sem,
    f_s,
    f_r,
    sib_s,
    sib_r,
    up_s,
    up_r,
    dn_s,
    dn_r,
    gsib_s,
    gsib_r,
    gup_s,
    gup_r,
    gdn_s,
    gdn_r,
    b_s,
    b_r,
    w0_s,
    w0_r,
    w1_s,
    w1_r,
    w2_s,
    w2_r,
    w3_s,
    w3_r,
    w4_s,
    w4_r,
    w5_s,
    w5_r,
):
    H = CHUNKS
    Z = C // 2
    T, F = feat.shape
    W = F // H
    slots = adj.shape[0] - 1
    i = lax.axis_index("row")
    j = lax.axis_index("col")
    z = j // 2
    c = lax.rem(j, 2)
    sibling = 2 * z + 1 - c
    pending = []

    def remote(src, dst, ssem, rsem, row, col):
        return pltpu.make_async_remote_copy(
            src_ref=src,
            dst_ref=dst,
            send_sem=ssem,
            recv_sem=rsem,
            device_id=(row, col),
            device_id_type=pl.DeviceIdType.MESH,
        )

    def send(copy, cond=None):
        if cond is None:
            copy.start()
        else:
            pl.when(cond)(copy.start)
        pending.append((copy, cond))

    adj_copy = pltpu.make_async_copy(adj_hbm.at[0, 0], adj.at[pl.ds(0, slots)], adj_sem)
    adj_copy.start()

    def tile_at(index):
        return pl.ds(pl.multiple_of(index * T, T), T)

    for h in range(H):
        feats[h, tile_at(i), :] = feat[:, pl.ds(h * W, W)]
    barrier = pltpu.get_barrier_semaphore()
    for q in range(1, R):
        pl.semaphore_signal(
            barrier, inc=1, device_id=(lax.rem(i + q, R), j), device_id_type=pl.DeviceIdType.MESH
        )
    for q in range(1, Z):
        pl.semaphore_signal(
            barrier,
            inc=1,
            device_id=(i, 2 * lax.rem(z + q, Z) + c),
            device_id_type=pl.DeviceIdType.MESH,
        )
    pl.semaphore_signal(
        barrier, inc=1, device_id=(i, sibling), device_id_type=pl.DeviceIdType.MESH
    )
    pl.semaphore_wait(barrier, R + Z - 1)

    def feat_copy(h, q):
        return remote(
            feats.at[h, tile_at(i), :],
            feats.at[h, tile_at(i), :],
            f_s.at[h, q - 1],
            f_r.at[h, q - 1],
            lax.rem(i + q, R),
            j,
        )

    for q in range(1, R):
        send(feat_copy(0, q))

    adj[slots] = jnp.zeros((T, T), BF)
    adj_copy.wait()
    count = count_s[0, 0]

    def fill(r, carry):
        for k in range(R):
            found = jnp.int32(slots)
            for t in range(slots):
                hit = (rows_s[0, 0, t] == r) & (cols_s[0, 0, t] == k) & (t < count)
                found = jnp.where(hit, jnp.int32(t), found)
            dense[tile_at(lax.rem(r, 2) * Z + r // 2), k * T : (k + 1) * T] = adj[found]
        return carry

    lax.fori_loop(0, C, fill, 0)

    step = min(Z, 4) * T

    def core_rows(core, first):
        return pl.ds(pl.multiple_of(core * Z * T + first, step), step)

    def sib_copy(h):
        return remote(sib_send.at[h], sib_recv.at[h], sib_s.at[h], sib_r.at[h], i, sibling)

    def forward(h):
        for q in range(1, R):
            feat_copy(h, q).wait_recv()
        if h + 1 < H:
            for q in range(1, R):
                send(feat_copy(h + 1, q))
        for first in range(0, Z * T, step):
            part = dot(dense[core_rows(1 - c, first), :], feats[h])
            sib_send[h, first : first + step] = part.astype(BF)
        send(sib_copy(h))
        for first in range(0, Z * T, step):
            part = dot(dense[core_rows(c, first), :], feats[h])
            if first == 0:
                sib_copy(h).wait_recv()
            part = part + sib_recv[h, first : first + step].astype(F32)
            chip[h, first : first + step] = part.astype(BF)

    above = jnp.minimum(z + 1, Z - 1)
    below = jnp.maximum(z - 1, 0)

    def up_copy(h, s):
        return remote(
            chip.at[h, pl.ds((Z - 1 - s) * T, T)], up_recv.at[h, s], up_s.at[h, s], up_r.at[h, s], i, 2 * above + c
        )

    def dn_copy(h, s):
        return remote(
            chip.at[h, pl.ds(s * T, T)], dn_recv.at[h, s], dn_s.at[h, s], dn_r.at[h, s], i, 2 * below + c
        )

    def chain(h, s):
        d = Z - 1 - s

        @pl.when((z > 0) & (z < d))
        def _():
            up_copy(h, s).wait_recv()
            chip[h, d * T : (d + 1) * T] = (chip[h, d * T : (d + 1) * T].astype(F32) + up_recv[h, s].astype(F32)).astype(BF)

        send(up_copy(h, s), z < d)

        @pl.when((z < Z - 1) & (z > s))
        def _():
            dn_copy(h, s).wait_recv()
            chip[h, s * T : (s + 1) * T] = (chip[h, s * T : (s + 1) * T].astype(F32) + dn_recv[h, s].astype(F32)).astype(BF)

        send(dn_copy(h, s), z > s)

    def finish(h):
        cols = pl.ds(h * W, W)

        @pl.when(z == 0)
        def _():
            dn_copy(h, z).wait_recv()
            agg[:, cols] = (chip[h, tile_at(z)].astype(F32) + dn_recv[h, z].astype(F32)).astype(BF)

        @pl.when(z == Z - 1)
        def _():
            up_copy(h, Z - 1 - z).wait_recv()
            agg[:, cols] = (chip[h, tile_at(z)].astype(F32) + up_recv[h, Z - 1 - z].astype(F32)).astype(BF)

        @pl.when((z > 0) & (z < Z - 1))
        def _():
            up_copy(h, Z - 1 - z).wait_recv()
            dn_copy(h, z).wait_recv()
            both = up_recv[h, Z - 1 - z].astype(F32) + dn_recv[h, z].astype(F32)
            agg[:, cols] = (chip[h, tile_at(z)].astype(F32) + both).astype(BF)

    for wave in range(H + Z - 2):
        for s in range(Z - 2, 0, -1):
            if 0 <= wave - s < H:
                chain(wave - s, s)
        if wave < H:
            forward(wave)
            chain(wave, 0)
    for h in range(H):
        finish(h)

    pre = dot(agg[...], weight[...])
    sigma = 1.0 / (1.0 + jnp.exp(-pre))
    dpre = (ngrad[...].astype(F32) * sigma * (1.0 + pre * (1.0 - sigma))).astype(BF)
    dpre_v[...] = dpre

    def gsib_copy(h, owner):
        r = c * Z + owner
        return remote(
            grads.at[h, r], grads.at[h, r], gsib_s.at[h, owner], gsib_r.at[h, owner],
            i, sibling,
        )

    def gup_copy(h, s):
        r = c * Z + jnp.maximum(z - s, 0)
        return remote(
            grads.at[h, r], grads.at[h, r], gup_s.at[h, s], gup_r.at[h, s],
            i, 2 * above + c,
        )

    def gdn_copy(h, s):
        r = c * Z + jnp.minimum(z + s, Z - 1)
        return remote(
            grads.at[h, r], grads.at[h, r], gdn_s.at[h, s], gdn_r.at[h, s],
            i, 2 * below + c,
        )

    turned = lax.dot_general(
        weight[...], dpre_v[...], (((1,), (1,)), ((), ())), preferred_element_type=F32
    ).astype(BF)
    for h in range(H):
        grads[h, c * Z + z] = turned[h * W : (h + 1) * W, :]

    def give(h):
        send(gup_copy(h, 0), z < Z - 1)
        send(gdn_copy(h, 0), z > 0)
        send(gsib_copy(h, z))

    give(0)
    out[...] = (pre * sigma).astype(BF)

    half = F // 2
    S1 = half // R
    groups = S1 // 16
    cg = Z // groups
    width = F // cg

    def slab_at(index):
        return pl.ds(pl.multiple_of(index * S1, S1), S1)

    def half_at(index):
        return pl.ds(pl.multiple_of(index * half, half), half)

    def piece_at(index):
        return (
            pl.ds(pl.multiple_of(index // cg * 16, 16), 16),
            pl.ds(pl.multiple_of(lax.rem(index, cg) * width, width), width),
        )

    w0_copy = remote(w0_send, w0_recv, w0_s, w0_r, i, sibling)

    def w1_copy(q):
        return remote(
            w1_send.at[q - 1], w1_recv.at[q - 1], w1_s.at[q - 1], w1_r.at[q - 1],
            lax.rem(i + q, R), j,
        )

    def w2_copy(q):
        return remote(
            w2_send.at[q - 1], w2_recv.at[q - 1], w2_s.at[q - 1], w2_r.at[q - 1],
            i, 2 * lax.rem(z + q, Z) + c,
        )

    def w3_copy(q, owner):
        r, k = piece_at(owner)
        return remote(
            wslab.at[r, k], wslab.at[r, k], w3_s.at[q - 1], w3_r.at[q - 1],
            i, 2 * lax.rem(z + q, Z) + c,
        )

    def w4_copy(q, owner):
        rows = slab_at(c * R + owner)
        return remote(
            wslab, wfull.at[rows, :], w4_s.at[q - 1], w4_r.at[q - 1], lax.rem(i + q, R), j
        )

    def w5_copy(core):
        rows = half_at(core)
        return remote(wfull.at[rows, :], wfull.at[rows, :], w5_s, w5_r, i, sibling)

    wterm[...] = (
        lax.dot_general(
            agg[...], dpre_v[...], (((0,), (0,)), ((), ())), preferred_element_type=F32
        )
        * scale
    )
    w0_send[...] = wterm[half_at(1 - c), :].astype(BF)
    send(w0_copy)

    def sum_pair():
        w0_copy.wait_recv()
        w_pair[...] = wterm[half_at(c), :] + w0_recv[...].astype(F32)
        for q in range(1, R):
            w1_send[q - 1] = w_pair[slab_at(lax.rem(i + q, R)), :].astype(BF)
            send(w1_copy(q))

    def sum_row():
        acc = w_pair[slab_at(i), :]
        for q in range(1, R):
            w1_copy(q).wait_recv()
            acc = acc + w1_recv[q - 1].astype(F32)
        w1_sum[...] = acc
        for q in range(1, Z):
            r, k = piece_at(lax.rem(z + q, Z))
            w2_send[q - 1] = w1_sum[r, k].astype(BF)
            send(w2_copy(q))

    def sum_chain():
        r, k = piece_at(z)
        acc = w1_sum[r, k]
        for q in range(1, Z):
            w2_copy(q).wait_recv()
            acc = acc + w2_recv[q - 1].astype(F32)
        wslab[r, k] = acc.astype(BF)
        for q in range(1, Z):
            send(w3_copy(q, z))

    def share_row():
        for q in range(1, Z):
            w3_copy(q, lax.rem(z - q + Z, Z)).wait_recv()
        for q in range(1, R):
            send(w4_copy(q, i))
        wfull[slab_at(c * R + i), :] = wslab[...]

    def share_pair():
        for q in range(1, R):
            w4_copy(q, lax.rem(i - q + R, R)).wait_recv()
        send(w5_copy(c))

    def gather(h, s):
        from_below = z - 1 - s >= 0
        from_above = z + 1 + s <= Z - 1

        @pl.when(from_below)
        def _():
            gup_copy(h, s).wait_recv()

        if s + 1 < Z - 1:
            send(gup_copy(h, s + 1), from_below & (z < Z - 1))
        send(gsib_copy(h, jnp.maximum(z - 1 - s, 0)), from_below)

        @pl.when(from_above)
        def _():
            gdn_copy(h, s).wait_recv()

        if s + 1 < Z - 1:
            send(gdn_copy(h, s + 1), from_above & (z > 0))
        send(gsib_copy(h, jnp.minimum(z + 1 + s, Z - 1)), from_above)

    def b_copy(h, q):
        return remote(
            b_send.at[h, q - 1], b_recv.at[h, q - 1], b_s.at[h, q - 1], b_r.at[h, q - 1],
            lax.rem(i + q, R), j,
        )

    def cell_cols(k):
        return dot(wide[...], dense[:, tile_at(k)])

    def backward(h):
        for d in range(Z):
            gsib_copy(h, d).wait_recv()
        for r in range(C):
            wide[:, r * T : (r + 1) * T] = grads[h, r]
        for q in range(1, R):
            b_send[h, q - 1] = cell_cols(lax.rem(i + q, R)).astype(BF)
            send(b_copy(h, q))
        b_own[h] = cell_cols(i)

    def total(h):
        acc = b_own[h]
        for q in range(1, R):
            b_copy(h, q).wait_recv()
            acc = acc + b_recv[h, q - 1].astype(F32)
        fgrad[:, h * W : (h + 1) * W] = acc.T.astype(BF)

    give(1)
    for wave in range(H + Z - 2):
        for s in range(Z - 2, -1, -1):
            if 0 <= wave - s < H:
                gather(wave - s, s)
        if wave + 2 < H:
            give(wave + 2)
        if wave == 0:
            sum_pair()
        if wave == 1:
            sum_row()
        h = wave - (Z - 2)
        if h == H - 1:
            share_row()
        if h >= 0:
            backward(h)
        if h == 0:
            sum_chain()
    for h in range(H - 1):
        total(h)
    share_pair()
    total(H - 1)
    w5_copy(1 - c).wait_recv()

    for copy, cond in pending:
        if cond is None:
            copy.wait_send()
        else:
            pl.when(cond)(copy.wait_send)


def hand_over(node_in, weight_in, feature_in, node_out, weight_out, feature_out):
    node_out[...] = node_in[...]
    weight_out[...] = weight_in[...].astype(F32)
    feature_out[...] = feature_in[...]


def local(adj_tiles, tile_rows, tile_cols, tile_counts, features, weight, node_grad):
    R = lax.axis_size("row")
    C = lax.axis_size("col")
    Z = C // 2
    H = CHUNKS
    T, F = features.shape
    W = F // H
    slots = adj_tiles.shape[2]
    S1 = F // 2 // R
    width = F // (Z // (S1 // 16))
    scale = float((T * R * C) ** -0.5)
    vmem = pltpu.VMEM
    dma = pltpu.SemaphoreType.DMA
    scratch = [
        vmem((slots + 1, T, T), BF),
        vmem((C * T, R * T), BF),
        vmem((H, R * T, W), BF),
        vmem((H, Z * T, W), BF),
        vmem((H, Z * T, W), BF),
        vmem((H, Z * T, W), BF),
        vmem((H, Z - 1, T, W), BF),
        vmem((H, Z - 1, T, W), BF),
        vmem((T, F), BF),
        vmem((T, F), BF),
        vmem((H, C, W, T), BF),
        vmem((W, C * T), BF),
        vmem((H, W, T), F32),
        vmem((H, R - 1, W, T), BF),
        vmem((H, R - 1, W, T), BF),
        vmem((F, F), F32),
        vmem((F // 2, F), BF),
        vmem((F // 2, F), BF),
        vmem((F // 2, F), F32),
        vmem((R - 1, S1, F), BF),
        vmem((R - 1, S1, F), BF),
        vmem((S1, F), F32),
        vmem((Z - 1, 16, width), BF),
        vmem((Z - 1, 16, width), BF),
        vmem((S1, F), BF),
        dma(()),
    ]
    for shape in (
        (H, R - 1),
        (H,),
        (H, Z - 1),
        (H, Z - 1),
        (H, Z),
        (H, Z - 1),
        (H, Z - 1),
        (H, R - 1),
        (),
        (R - 1,),
        (Z - 1,),
        (Z - 1,),
        (R - 1,),
        (),
    ):
        scratch += [dma(shape), dma(shape)]
    whole = pl.BlockSpec(memory_space=pltpu.VMEM)
    scalars = pl.BlockSpec(memory_space=pltpu.SMEM)
    node_out, weight_grad, feature_grad = pl.pallas_call(
        functools.partial(kernel, R, C, scale),
        out_shape=(
            jax.ShapeDtypeStruct((T, F), BF),
            jax.ShapeDtypeStruct((F, F), BF),
            jax.ShapeDtypeStruct((T, F), BF),
        ),
        in_specs=[scalars] * 3 + [pl.BlockSpec(memory_space=pl.ANY)] + [whole] * 3,
        out_specs=(whole, whole, whole),
        scratch_shapes=scratch,
        compiler_params=pltpu.CompilerParams(
            collective_id=0, has_side_effects=True, vmem_limit_bytes=62 * 1024 * 1024
        ),
        name="layer",
    )(tile_rows, tile_cols, tile_counts, adj_tiles, features, weight, node_grad)
    return pl.pallas_call(
        hand_over,
        out_shape=(
            jax.ShapeDtypeStruct((T, F), BF),
            jax.ShapeDtypeStruct((F, F), F32),
            jax.ShapeDtypeStruct((T, F), BF),
        ),
        in_specs=[whole] * 3,
        out_specs=(whole, whole, whole),
        name="hand_over",
    )(node_out, weight_grad, feature_grad)


def solution(mesh):
    in_specs = (
        P("row", "col", None, None, None),
        P("row", "col", None),
        P("row", "col", None),
        P("row", "col"),
        P(("col", "row"), None),
        P(),
        P(("row", "col"), None),
    )
    out_specs = (P(("row", "col"), None), P(), P(("col", "row"), None))
    return jax.shard_map(local, mesh=mesh, in_specs=in_specs, out_specs=out_specs, check_vma=False)
```
